32 devices in a mesh: dp: 8 (over z, x), tensor: 4 (over y, core).
Axes of the slice: x: 2, y: 2, z: 4, core: 2. Of those that a mesh axis runs over, the one named last changes fastest.
Arguments:
- queries: bfloat16 [2048, 4096], P('dp', 'tensor'), may hold values from -6 to 6
- span_keys: bfloat16 [2048, 1024], P('dp', 'tensor'), may hold values from -6 to 6
- span_values: bfloat16 [2048, 1024], P('dp', 'tensor'), may hold values from -6 to 6
- cache_keys: bfloat16 [2048, 1024], P(None, 'tensor'), may hold values from -6 to 6
- cache_values: bfloat16 [2048, 1024], P(None, 'tensor'), may hold values from -6 to 6
- out_proj: bfloat16 [4096, 8192], P('tensor'), may hold values from -0.09375 to 0.09375
- out_grad: bfloat16 [2048, 8192], P('dp', 'tensor'), may hold values from -6 to 6
- doc_ids: int32 [8, 256], P('dp'), may hold values from 0 to 15, never falling along the last dimension, each value on 1 to 128 neighbouring positions
Outputs:
- attended: bfloat16 [2048, 4096], P('dp', 'tensor')
- new_keys: float32 [2048, 1024], P('dp', 'tensor')
- new_values: float32 [2048, 1024], P('dp', 'tensor')
The draws below stay inside these ranges and needn't reach their ends.
All inputs are finite; a program needn't handle non-finite values.
Results may differ from the reference program's by a relative error of at most 0.0055.
Values may be sent and summed in bfloat16 or wider, within the bound.
No kernel may reach another device: no remote copies, remote signals or barrier semaphores. Data moves between devices by JAX's collectives and lax.ppermute only.
A program may use at most 192 MiB of HBM per device.

```python
import math
import jax
import jax.numpy as jnp
import numpy as np
from jax import lax

D = 8192
HD = 128
KVH = 8
QH = 32
SLOTS = 2048
LEN = 256
SEQS = 8
TOKENS = 2048


def draw_queries(key, part):
    key = jax.random.fold_in(key, 11)
    values = jnp.clip(jax.random.normal(key, (TOKENS, QH * HD), jnp.float32), -6.0, 6.0)
    return values.astype(jnp.bfloat16)


def draw_cache_keys(key, part):
    key = jax.random.fold_in(key, 12)
    values = jnp.clip(jax.random.normal(key, (SLOTS, KVH * HD), jnp.float32), -6.0, 6.0)
    return values.astype(jnp.bfloat16)


def level_of(rng, dims, shards, least, top_value):
    def one(position, blocks):
        heights = jax.random.uniform(jax.random.fold_in(jax.random.fold_in(rng, 6), position), (blocks,), jnp.float32, least / len(shards), top_value / len(shards))
        return jnp.repeat(jnp.exp(heights), dims[position] // blocks).reshape((-1,) + (1,) * (len(dims) - position - 1))

    level = one(*shards[0])
    for cut in shards[1:]:
        level = level * one(*cut)
    return level


def length_profile(count, total, bound, slope):
    weights = [(1 << 20) // math.isqrt(standing ** slope) + 1 for standing in range(2, count + 1)]
    rest, holding = total - bound - (count - 1), [1] * (count - 1)
    while rest > 0:
        movable = [i for i in range(count - 1) if holding[i] < bound]
        pool, remaining = sum([weights[i] for i in movable]), rest
        for i in movable:
            extra = min(bound - holding[i], max(1, remaining * weights[i] // pool), rest)
            holding[i] = holding[i] + extra
            rest = rest - extra
    return np.array([bound] + holding)


def ragged(key, count, total, limit, lean):
    if count == 2:
        one = jax.random.randint(key, (), max(1, total - limit), min(limit, total - 1) + 1)
        return jnp.stack([one, total - one])
    sizes = jnp.asarray(length_profile(count, total, limit, lean), jnp.int32)
    twos = (count - 1) // 2
    donor, taker = sizes[1:1 + 2 * twos:2], sizes[2:2 + 2 * twos:2]
    margin = jnp.minimum(donor - 1, limit - taker)
    moved = jax.random.randint(jax.random.fold_in(key, 1), (twos,), 0, 1 << 20) % (margin + 1)
    sizes = sizes.at[1:1 + 2 * twos:2].set(donor - moved).at[2:2 + 2 * twos:2].set(taker + moved)
    return sizes[jax.random.permutation(jax.random.fold_in(key, 2), count)]


def normal_values(own_key, extent, scale, most, shards=(), kind=jnp.bfloat16):
    factor_of = level_of(own_key, extent, shards, -0.22, 0.18) if shards else 1.0
    drawn = jax.random.normal(own_key, extent, jnp.float32) * scale * factor_of
    return jnp.minimum(jnp.maximum(drawn, -most), most).astype(kind)


def setup_inputs(seed: int = 0) -> dict:
    splits = jax.random.split(jax.random.key(seed), 9)
    return {
        "queries": draw_queries(jax.random.fold_in(splits[8], 71), 0),
        "span_keys": normal_values(splits[1], (TOKENS, KVH * HD), 1.0, 6.0, ((0, 8), (1, 4))),
        "span_values": normal_values(splits[2], (TOKENS, KVH * HD), 1.0, 6.0, ((0, 8), (1, 4))),
        "cache_keys": draw_cache_keys(jax.random.fold_in(splits[8], 71), 0),
        "cache_values": normal_values(splits[4], (SLOTS, KVH * HD), 1.0, 6.0, ((1, 4),)),
        "out_proj": normal_values(splits[5], (QH * HD, D), (QH * HD) ** -0.5, 0.09375, ((0, 4),)),
        "out_grad": normal_values(splits[6], (TOKENS, D), 1.0, 6.0, ((0, 8), (1, 4))),
        "doc_ids": jax.vmap(lambda own: jnp.searchsorted(jnp.cumsum(ragged(own, max(4, LEN // 16), LEN, LEN // 2, 2)), jnp.arange(LEN), side="right"))(jax.random.split(splits[7], SEQS)).reshape((SEQS, LEN)).astype(jnp.int32),
    }


step_rate = 0.25
epsilon = 1e-06

def seq_terms(query_rows, span_k, span_v, seq_docs, cache_k, cache_v, grad_att):
    length = query_rows.shape[0]
    slots = cache_k.shape[0]
    kv_heads = cache_k.shape[1] // HD
    group = query_rows.shape[1] // (kv_heads * HD)
    scale_factor = 1.0 / math.sqrt(HD)
    query_four = query_rows.astype(jnp.float32).reshape(length, kv_heads, group, HD)
    all_keys = jnp.concatenate([cache_k, span_k], 0).astype(jnp.float32).reshape(slots + length, kv_heads, HD)
    all_vals = jnp.concatenate([cache_v, span_v], 0).astype(jnp.float32).reshape(slots + length, kv_heads, HD)
    scores = jnp.einsum('tgjd,kgd->gjtk', query_four, all_keys) * scale_factor
    places = jnp.arange(length)
    span_ok = (seq_docs[None, :] == seq_docs[:, None]) & (places[None, :] <= places[:, None])
    allowed = jnp.concatenate([jnp.ones((length, slots), bool), span_ok], 1)
    scores = jnp.where(allowed, scores, -1e+30)
    highest = lax.optimization_barrier(jnp.max(scores, -1, keepdims=True))
    expo = jnp.exp(scores - highest)
    probs = expo / lax.optimization_barrier(jnp.sum(expo, -1, keepdims=True))
    probs_b = probs.astype(jnp.bfloat16)
    attended = jnp.einsum('gjtk,kgd->tgjd', probs_b.astype(jnp.float32), all_vals).astype(jnp.bfloat16)
    grad_four = grad_att.astype(jnp.float32).reshape(length, kv_heads, group, HD)
    grad_probs = jnp.einsum('tgjd,kgd->gjtk', grad_four, all_vals)
    row_dot = lax.optimization_barrier(jnp.sum(grad_four * attended.astype(jnp.float32), -1)).transpose(1, 2, 0)
    grad_scores = (probs * (grad_probs - row_dot[..., None])).astype(jnp.bfloat16)
    grad_keys = jnp.einsum('gjtk,tgjd->kgd', grad_scores.astype(jnp.float32)[..., :slots], query_four) * scale_factor
    grad_vals = jnp.einsum('gjtk,tgjd->kgd', probs_b.astype(jnp.float32)[..., :slots], grad_four)
    return (attended.reshape(length, -1), grad_keys.reshape(slots, -1), grad_vals.reshape(slots, -1))

def reference(queries, span_keys, span_values, cache_keys, cache_values, out_proj, out_grad, doc_ids):
    grad_att = jnp.dot(out_grad, out_proj.T, preferred_element_type=jnp.float32).astype(jnp.bfloat16)
    inputs = (queries.reshape(SEQS, LEN, -1), span_keys.reshape(SEQS, LEN, -1), span_values.reshape(SEQS, LEN, -1), doc_ids, grad_att.reshape(SEQS, LEN, -1))

    def one_seq(running, pieces):
        query_rows, span_k, span_v, seq_docs, grad_rows = pieces
        attended, grad_keys, grad_vals = seq_terms(query_rows, span_k, span_v, seq_docs, cache_keys, cache_values, grad_rows)
        return ((running[0] + grad_keys, running[1] + grad_vals), attended)
    zeros_grad = jnp.zeros((SLOTS, KVH * HD), jnp.float32)
    (grad_keys, grad_vals), attended = lax.scan(one_seq, (zeros_grad, zeros_grad), inputs)
    total = (jnp.sum(grad_keys * grad_keys) + jnp.sum(grad_vals * grad_vals)) / (2 * SLOTS * KVH * HD)
    rms_value = jnp.sqrt(total + epsilon)
    new_keys = cache_keys.astype(jnp.float32) - step_rate * grad_keys / rms_value
    new_values = cache_values.astype(jnp.float32) - step_rate * grad_vals / rms_value
    return (attended.reshape(TOKENS, -1), new_keys, new_values)
```

```python
import functools
import math

import jax
import jax.numpy as jnp
from jax import lax
from jax.experimental import pallas as pl
from jax.experimental.pallas import tpu as pltpu
from jax.sharding import PartitionSpec as P

HD = 128
KVH = 8
SLOTS = 2048

step_rate = 0.25
epsilon = 1e-06

F32 = jnp.float32
BF16 = jnp.bfloat16
NT = (((1,), (1,)), ((), ()))
NN = (((1,), (0,)), ((), ()))
TN = (((0,), (0,)), ((), ()))
MIB = 1 << 20


def mm(a, b, dims):
    return lax.dot_general(a, b, dims, preferred_element_type=F32)


def bit_orders(n, heads):
    bits = max(1, n.bit_length() - 1)
    first = list(range(bits))
    if n == 1:
        return [[] for _ in range(heads)]
    second = first[:]
    if bits > 1:
        second[0], second[1] = second[1], second[0]
    return [first if head % 2 == 0 else second for head in range(heads)]


def place_of(rel, order):
    place = 0
    for step, bit in enumerate(order):
        place = place + (((rel >> bit) & 1) << (len(order) - 1 - step))
    return place


def block_at(place, order):
    rel = 0
    for step, bit in enumerate(order):
        rel = rel + (((place >> (len(order) - 1 - step)) & 1) << bit)
    return rel


def per_head(g, orders, fn):
    even = fn(orders[0])
    if len(orders) == 1:
        return even
    return jnp.where(g % 2 == 0, even, fn(orders[1]))


def forward_kernel(orders, n, me_ref, q_ref, k_ref, ks_ref, v_ref, vs_ref, bias_ref, p_ref, att_ref, att_t_ref, s_ref):
    g = pl.program_id(0)
    me = me_ref[0]
    slots = k_ref.shape[0]
    length = q_ref.shape[0]
    share = slots // n
    chunk = 256
    scale = math.log2(math.e) / math.sqrt(HD)
    q = q_ref[...]
    steps = [(k_ref, v_ref, c, c, chunk) for c in range(0, slots, chunk)]
    steps.append((ks_ref, vs_ref, 0, slots, length))
    high = None
    for keys, _, at, row, size in steps:
        s = mm(keys[at : at + size, :], q, NT) * scale
        if keys is ks_ref:
            s = s + bias_ref[...]
        s_ref[row : row + size, :] = s
        top = jnp.max(s.reshape(size // 8, 8, length), axis=0)
        high = top if high is None else jnp.maximum(high, top)
    high = jnp.max(high, axis=0, keepdims=True)
    total = None
    for _, _, _, row, size in steps:
        e = jnp.exp2(s_ref[row : row + size, :] - high)
        s_ref[row : row + size, :] = e
        part = jnp.sum(e.reshape(size // 8, 8, length), axis=0)
        total = part if total is None else total + part
    inverse = 1.0 / jnp.sum(total, axis=0, keepdims=True)
    att = None
    for keys, values, at, row, size in steps:
        p = (s_ref[row : row + size, :] * inverse).astype(BF16)
        if keys is k_ref:
            piece = min(share, size)
            for b in range(0, size, piece):
                block, inside = (at + b) // share, (at + b) % share
                place = per_head(g, orders, functools.partial(place_of, block ^ me))
                start = pl.multiple_of(place * share + inside, piece)
                p_ref[0, 0, pl.ds(start, piece), :] = p[b : b + piece, :]
        part = mm(values[at : at + size, :], p, TN)
        att = part if att is None else att + part
    att_t_ref[...] = att.astype(BF16)
    att_ref[...] = att.T.astype(BF16)


def forward(me, queries, cache_k, span_k, cache_v, span_v, bias, orders, n):
    length, width = queries.shape
    slots, kv_width = cache_k.shape
    kv = kv_width // HD
    group = width // kv_width
    spec = pltpu.PrefetchScalarGridSpec(
        num_scalar_prefetch=1,
        grid=(kv, group),
        in_specs=[
            pl.BlockSpec((length, HD), lambda g, j, me: (0, g * group + j)),
            pl.BlockSpec((slots, HD), lambda g, j, me: (0, g)),
            pl.BlockSpec((length, HD), lambda g, j, me: (0, g)),
            pl.BlockSpec((slots, HD), lambda g, j, me: (0, g)),
            pl.BlockSpec((length, HD), lambda g, j, me: (0, g)),
            pl.BlockSpec((length, length), lambda g, j, me: (0, 0)),
        ],
        out_specs=[
            pl.BlockSpec((1, 1, slots, length), lambda g, j, me: (g, j, 0, 0)),
            pl.BlockSpec((length, HD), lambda g, j, me: (0, g * group + j)),
            pl.BlockSpec((HD, length), lambda g, j, me: (g * group + j, 0)),
        ],
        scratch_shapes=[pltpu.VMEM((slots + length, length), F32)],
    )
    return pl.pallas_call(
        functools.partial(forward_kernel, orders, n),
        grid_spec=spec,
        out_shape=[
            jax.ShapeDtypeStruct((kv, group, slots, length), BF16),
            jax.ShapeDtypeStruct((length, width), BF16),
            jax.ShapeDtypeStruct((width, length), BF16),
        ],
        compiler_params=pltpu.CompilerParams(vmem_limit_bytes=32 * MIB),
        cost_estimate=pl.CostEstimate(
            flops=4 * width * length * (slots + length),
            bytes_accessed=2 * width // HD * length * slots,
            transcendentals=width // HD * length * (slots + length),
        ),
        name="forward",
    )(me, queries, cache_k, span_k, cache_v, span_v, bias)


def project_kernel(first, shard_ref, w_ref, g_ref, *refs):
    out_ref = refs[-1]
    total = mm(w_ref[...], g_ref[...], NT)
    if not first:
        total = total + refs[0][...]
    out_ref[...] = total.astype(out_ref.dtype)


def project(shard, out_proj, grad, acc, dtype):
    rows = out_proj.shape[0]
    length, features = grad.shape
    block = min(256, rows)
    in_specs = [
        pl.BlockSpec((block, features), lambda m, shard: (m, shard[0])),
        pl.BlockSpec((length, features), lambda m, shard: (0, 0)),
    ]
    args = [out_proj, grad]
    if acc is not None:
        in_specs.append(pl.BlockSpec((block, length), lambda m, shard: (m, 0)))
        args.append(acc)
    return pl.pallas_call(
        functools.partial(project_kernel, acc is None),
        grid_spec=pltpu.PrefetchScalarGridSpec(
            num_scalar_prefetch=1,
            grid=(rows // block,),
            in_specs=in_specs,
            out_specs=pl.BlockSpec((block, length), lambda m, shard: (m, 0)),
        ),
        out_shape=jax.ShapeDtypeStruct((rows, length), dtype),
        compiler_params=pltpu.CompilerParams(vmem_limit_bytes=32 * MIB),
        cost_estimate=pl.CostEstimate(
            flops=2 * rows * length * features,
            bytes_accessed=2 * rows * features,
            transcendentals=0,
        ),
        name="project",
    )(shard.reshape(1), *args)


def values_kernel(p_ref, da_ref, out_ref):
    total = None
    for j in range(p_ref.shape[1]):
        part = mm(p_ref[0, j], da_ref[j * HD : (j + 1) * HD, :], NT)
        total = part if total is None else total + part
    out_ref[...] = total.astype(BF16)


def value_grads(head, probs, grad_att_t):
    _, group, slots, length = probs.shape
    rows = 512
    return pl.pallas_call(
        values_kernel,
        grid=(slots // rows,),
        in_specs=[
            pl.BlockSpec((1, group, rows, length), lambda i: (head, 0, i, 0)),
            pl.BlockSpec((group * HD, length), lambda i: (head, 0)),
        ],
        out_specs=pl.BlockSpec((rows, HD), lambda i: (i, 0)),
        out_shape=jax.ShapeDtypeStruct((slots, HD), BF16),
        compiler_params=pltpu.CompilerParams(vmem_limit_bytes=32 * MIB),
        cost_estimate=pl.CostEstimate(
            flops=2 * slots * length * group * HD,
            bytes_accessed=2 * slots * length * group,
            transcendentals=0,
        ),
        name="value_grads",
    )(probs, grad_att_t)


def keys_kernel(order, n, me_ref, p_ref, v_ref, da_ref, att_ref, q_ref, out_ref, dot_ref):
    i = pl.program_id(0)
    me = me_ref[0]
    group, rows = p_ref.shape[1], p_ref.shape[2]
    share = v_ref.shape[0] // n
    piece = min(share, rows)

    @pl.when(i == 0)
    def _():
        for j in range(group):
            cut = slice(j * HD, (j + 1) * HD)
            product = da_ref[cut, :].astype(F32) * att_ref[cut, :].astype(F32)
            dot_ref[j : j + 1, :] = jnp.sum(product, axis=0, keepdims=True)

    for b in range(0, rows, piece):
        row = i * rows + b
        place, inside = row // share, row % share
        block = block_at(place, order) ^ me
        start = pl.multiple_of(block * share + inside, piece)
        values = v_ref[pl.ds(start, piece), :]
        total = None
        for j in range(group):
            grad_p = mm(values, da_ref[j * HD : (j + 1) * HD, :], NN)
            p = p_ref[0, j, b : b + piece, :].astype(F32)
            grad_s = (p * (grad_p - dot_ref[j : j + 1, :])).astype(BF16)
            part = mm(grad_s, q_ref[:, j * HD : (j + 1) * HD], NN)
            total = part if total is None else total + part
        out_ref[b : b + piece, :] = (total * (1.0 / math.sqrt(HD))).astype(BF16)


def key_grads(head, me, probs, cache_v, grad_att_t, att_t, queries, order, n):
    _, group, slots, length = probs.shape
    rows = 512
    return pl.pallas_call(
        functools.partial(keys_kernel, order, n),
        grid_spec=pltpu.PrefetchScalarGridSpec(
            num_scalar_prefetch=1,
            grid=(slots // rows,),
            in_specs=[
                pl.BlockSpec((1, group, rows, length), lambda i, me: (head, 0, i, 0)),
                pl.BlockSpec((slots, HD), lambda i, me: (0, head)),
                pl.BlockSpec((group * HD, length), lambda i, me: (head, 0)),
                pl.BlockSpec((group * HD, length), lambda i, me: (head, 0)),
                pl.BlockSpec((length, group * HD), lambda i, me: (0, head)),
            ],
            out_specs=pl.BlockSpec((rows, HD), lambda i, me: (i, 0)),
            scratch_shapes=[pltpu.VMEM((max(8, group), length), F32)],
        ),
        out_shape=jax.ShapeDtypeStruct((slots, HD), BF16),
        compiler_params=pltpu.CompilerParams(vmem_limit_bytes=32 * MIB),
        cost_estimate=pl.CostEstimate(
            flops=4 * slots * length * group * HD,
            bytes_accessed=2 * slots * length * group,
            transcendentals=0,
        ),
        name="key_grads",
    )(me, probs, cache_v, grad_att_t, att_t, queries)


def exchange(value, axis, size, flip):
    return lax.ppermute(value, axis, [(i, i ^ flip) for i in range(size)])


def reduce_halving(part, order, n):
    for bit in order:
        half = part.shape[0] // 2
        got = exchange(part[half:], "dp", n, 1 << bit)
        total = part[:half].astype(F32) + got.astype(F32)
        part = total.astype(BF16)
    return total if order else part.astype(F32)


def body(queries, span_keys, span_values, cache_keys, cache_values, out_proj, out_grad, doc_ids):
    n = lax.axis_size("dp")
    t = lax.axis_size("tensor")
    mine = lax.axis_index("dp")
    shard = lax.axis_index("tensor")
    me = mine.astype(jnp.int32).reshape(1)
    length = queries.shape[0]
    kv = cache_keys.shape[1] // HD
    share = cache_keys.shape[0] // n
    orders = bit_orders(n, kv)

    far = [(exchange(out_grad, "tensor", t, 2 * s), 2 * s) for s in range(1, t // 2)]
    near = exchange(out_grad, "tensor", t, 1)

    docs = doc_ids[0]
    places = jnp.arange(length)
    span_ok = (docs[None, :] == docs[:, None]) & (places[:, None] <= places[None, :])
    bias = jnp.where(span_ok, 0.0, -1e30).astype(F32)
    probs, attended, att_t = forward(
        me, queries, cache_keys, span_keys, cache_values, span_values, bias, orders, n
    )

    acc = project(shard, out_proj, out_grad, None, F32)
    acc = project(shard ^ 1, out_proj, near, acc, F32)
    later = [(exchange(got, "tensor", t, 1), flip + 1) for got, flip in far]
    pieces = [pair for both in zip(far, later) for pair in both]
    for place, (got, flip) in enumerate(pieces):
        last = place == len(pieces) - 1
        acc = project(shard ^ flip, out_proj, got, acc, BF16 if last else F32)

    grads_v = [
        reduce_halving(value_grads(h, probs, acc), orders[h], n) for h in range(kv)
    ]
    grads_k = [
        reduce_halving(
            key_grads(h, me, probs, cache_values, acc, att_t, queries, orders[h], n), orders[h], n
        )
        for h in range(kv)
    ]
    share_keys = jnp.concatenate(grads_k, axis=1)
    share_vals = jnp.concatenate(grads_v, axis=1)
    squares = jnp.sum(share_keys * share_keys) + jnp.sum(share_vals * share_vals)
    spread = jnp.broadcast_to(squares, (n * t, 8, 128))
    spread = lax.all_to_all(spread, ("dp", "tensor"), split_axis=0, concat_axis=0, tiled=True)
    total = jnp.sum(spread[:, 0, 0])
    count = 2 * SLOTS * KVH * HD
    rms_value = jnp.sqrt(total / count + epsilon)
    offset = mine * share
    own_keys = lax.dynamic_slice_in_dim(cache_keys, offset, share, 0).astype(F32)
    own_vals = lax.dynamic_slice_in_dim(cache_values, offset, share, 0).astype(F32)
    new_keys = own_keys - step_rate * share_keys / rms_value
    new_values = own_vals - step_rate * share_vals / rms_value
    return (attended, new_keys, new_values)


def solution(mesh):
    placed = (
        P("dp", "tensor"),
        P("dp", "tensor"),
        P("dp", "tensor"),
        P(None, "tensor"),
        P(None, "tensor"),
        P("tensor", None),
        P("dp", "tensor"),
        P("dp", None),
    )
    return jax.shard_map(
        body,
        mesh=mesh,
        in_specs=placed,
        out_specs=(P("dp", "tensor"), P("dp", "tensor"), P("dp", "tensor")),
        check_vma=False,
    )
```

```python
import functools
import math

import jax
import jax.numpy as jnp
from jax import lax
from jax.experimental import pallas as pl
from jax.experimental.pallas import tpu as pltpu
from jax.sharding import PartitionSpec as P

HD = 128
KVH = 8
SLOTS = 2048

step_rate = 0.25
epsilon = 1e-06

F32 = jnp.float32
BF16 = jnp.bfloat16
NT = (((1,), (1,)), ((), ()))
NN = (((1,), (0,)), ((), ()))
TN = (((0,), (0,)), ((), ()))
MIB = 1 << 20


def mm(a, b, dims):
    return lax.dot_general(a, b, dims, preferred_element_type=F32)


def bit_orders(n, heads):
    bits = max(1, n.bit_length() - 1)
    first = list(range(bits))
    if n == 1:
        return [[] for _ in range(heads)]
    second = first[:]
    if bits > 1:
        second[0], second[1] = second[1], second[0]
    return [first if head % 2 == 0 else second for head in range(heads)]


def place_of(rel, order):
    place = 0
    for step, bit in enumerate(order):
        place = place + (((rel >> bit) & 1) << (len(order) - 1 - step))
    return place


def block_at(place, order):
    rel = 0
    for step, bit in enumerate(order):
        rel = rel + (((place >> (len(order) - 1 - step)) & 1) << bit)
    return rel


def per_head(g, orders, fn):
    even = fn(orders[0])
    if len(orders) == 1:
        return even
    return jnp.where(g % 2 == 0, even, fn(orders[1]))


def forward_kernel(
    orders, n, me_ref, q_ref, k_ref, ks_ref, v_ref, vs_ref, bias_ref, w_ref,
    p_ref, att_ref, att_t_ref, held_ref, s_ref, sems,
):
    g, j = pl.program_id(0), pl.program_id(1)
    cut = w_ref.shape[0] // 4
    copies = [
        pltpu.make_async_copy(
            w_ref.at[c * cut : (c + 1) * cut], held_ref.at[c * cut : (c + 1) * cut], sems.at[c]
        )
        for c in range(4)
    ]

    @pl.when((g == 0) & (j == 0))
    def _():
        for copy in copies:
            copy.start()

    me = me_ref[0]
    slots = k_ref.shape[0]
    length = q_ref.shape[0]
    share = slots // n
    chunk = 256
    scale = math.log2(math.e) / math.sqrt(HD)
    q = q_ref[...]
    steps = [(k_ref, v_ref, c, c, chunk) for c in range(0, slots, chunk)]
    steps.append((ks_ref, vs_ref, 0, slots, length))
    high = None
    for keys, _, at, row, size in steps:
        s = mm(keys[at : at + size, :], q, NT) * scale
        if keys is ks_ref:
            s = s + bias_ref[...]
        s_ref[row : row + size, :] = s
        top = jnp.max(s.reshape(size // 8, 8, length), axis=0)
        high = top if high is None else jnp.maximum(high, top)
    high = jnp.max(high, axis=0, keepdims=True)
    total = None
    for _, _, _, row, size in steps:
        e = jnp.exp2(s_ref[row : row + size, :] - high)
        s_ref[row : row + size, :] = e
        part = jnp.sum(e.reshape(size // 8, 8, length), axis=0)
        total = part if total is None else total + part
    inverse = 1.0 / jnp.sum(total, axis=0, keepdims=True)
    att = None
    for keys, values, at, row, size in steps:
        p = (s_ref[row : row + size, :] * inverse).astype(BF16)
        if keys is k_ref:
            piece = min(share, size)
            for b in range(0, size, piece):
                block, inside = (at + b) // share, (at + b) % share
                place = per_head(g, orders, functools.partial(place_of, block ^ me))
                start = pl.multiple_of(place * share + inside, piece)
                p_ref[0, pl.ds(start, piece), :] = p[b : b + piece, :]
        part = mm(values[at : at + size, :], p, TN)
        att = part if att is None else att + part
    att_t_ref[0] = att.astype(BF16)
    att_ref[...] = att.T.astype(BF16)

    @pl.when((g == pl.num_programs(0) - 1) & (j == pl.num_programs(1) - 1))
    def _():
        for copy in copies:
            copy.wait()


def forward(me, queries, cache_k, span_k, cache_v, span_v, bias, weights, orders, n):
    length, width = queries.shape
    slots, kv_width = cache_k.shape
    kv = kv_width // HD
    group = width // kv_width
    spec = pltpu.PrefetchScalarGridSpec(
        num_scalar_prefetch=1,
        grid=(kv, group),
        in_specs=[
            pl.BlockSpec((length, HD), lambda g, j, me: (0, g * group + j)),
            pl.BlockSpec((slots, HD), lambda g, j, me: (0, g)),
            pl.BlockSpec((length, HD), lambda g, j, me: (0, g)),
            pl.BlockSpec((slots, HD), lambda g, j, me: (0, g)),
            pl.BlockSpec((length, HD), lambda g, j, me: (0, g)),
            pl.BlockSpec((length, length), lambda g, j, me: (0, 0)),
            pl.BlockSpec(memory_space=pl.ANY),
        ],
        out_specs=[
            pl.BlockSpec((1, slots, length), lambda g, j, me: (g, 0, j)),
            pl.BlockSpec((length, HD), lambda g, j, me: (0, g * group + j)),
            pl.BlockSpec((1, HD, length), lambda g, j, me: (g, 0, j)),
            pl.BlockSpec(memory_space=pltpu.VMEM),
        ],
        scratch_shapes=[pltpu.VMEM((slots + length, length), F32), pltpu.SemaphoreType.DMA((4,))],
    )
    return pl.pallas_call(
        functools.partial(forward_kernel, orders, n),
        grid_spec=spec,
        out_shape=[
            jax.ShapeDtypeStruct((kv, slots, group * length), BF16),
            jax.ShapeDtypeStruct((length, width), BF16),
            jax.ShapeDtypeStruct((kv, HD, group * length), BF16),
            jax.ShapeDtypeStruct(weights.shape, BF16),
        ],
        compiler_params=pltpu.CompilerParams(vmem_limit_bytes=16 * MIB),
        cost_estimate=pl.CostEstimate(
            flops=4 * width * length * (slots + length),
            bytes_accessed=2 * width // HD * length * slots,
            transcendentals=width // HD * length * (slots + length),
        ),
        name="forward",
    )(me, queries, cache_k, span_k, cache_v, span_v, bias, weights)


def project_kernel(adds, heads, shard_ref, w_ref, g_ref, *refs):
    acc_ref, out_ref = refs if adds else (None, refs[0])
    rows, features = w_ref.shape[0], g_ref.shape[1]
    block = min(256, rows)
    columns = pl.ds(pl.multiple_of(shard_ref[0] * features, features), features)
    for m in range(0, rows, block):
        total = mm(w_ref[m : m + block, columns], g_ref[...], NT)
        if adds:
            total = total + acc_ref[m : m + block, :]
        if not heads:
            out_ref[m : m + block, :] = total
            continue
        length = total.shape[1]
        for b in range(0, block, HD):
            head = (m + b) // HD
            at = head % heads * length
            out_ref[head // heads, :, at : at + length] = total[b : b + HD, :].astype(BF16)


def project(shard, out_proj, grad, acc=None, heads=0):
    rows = out_proj.shape[0]
    length, features = grad.shape
    vmem = pl.BlockSpec(memory_space=pltpu.VMEM)
    args = [shard, out_proj, grad] + ([] if acc is None else [acc])
    if heads:
        out = jax.ShapeDtypeStruct((rows // HD // heads, HD, heads * length), BF16)
    else:
        out = jax.ShapeDtypeStruct((rows, length), F32)
    return pl.pallas_call(
        functools.partial(project_kernel, acc is not None, heads),
        in_specs=[pl.BlockSpec(memory_space=pltpu.SMEM)] + [vmem] * (len(args) - 1),
        out_specs=vmem,
        out_shape=out,
        compiler_params=pltpu.CompilerParams(vmem_limit_bytes=8 * MIB),
        cost_estimate=pl.CostEstimate(
            flops=2 * rows * length * features,
            bytes_accessed=2 * rows * features,
            transcendentals=0,
        ),
        name="project",
    )(*args)


def values_kernel(head, p_ref, da_ref, out_ref):
    rows = 256
    da = da_ref[head]
    for at in range(0, p_ref.shape[1], rows):
        out_ref[at : at + rows, :] = mm(p_ref[head, at : at + rows, :], da, NT).astype(BF16)


def value_grads(head, probs, grad_att_t):
    _, slots, wide = probs.shape
    vmem = pl.BlockSpec(memory_space=pltpu.VMEM)
    return pl.pallas_call(
        functools.partial(values_kernel, head),
        in_specs=[vmem, vmem],
        out_specs=vmem,
        out_shape=jax.ShapeDtypeStruct((slots, HD), BF16),
        compiler_params=pltpu.CompilerParams(vmem_limit_bytes=14 * MIB),
        cost_estimate=pl.CostEstimate(
            flops=2 * slots * wide, bytes_accessed=2 * slots * HD, transcendentals=0
        ),
        name="value_grads",
    )(probs, grad_att_t)


def keys_kernel(head, order, n, me_ref, p_ref, v_ref, da_ref, att_ref, q_ref, out_ref):
    me = me_ref[0]
    slots = p_ref.shape[1]
    share = slots // n
    length = q_ref.shape[0]
    group = p_ref.shape[2] // length
    piece = min(share, 256)
    da = da_ref[head]
    dot = jnp.sum(da.astype(F32) * att_ref[head].astype(F32), axis=0, keepdims=True)
    first = head * group * HD
    q = jnp.concatenate(
        [q_ref[:, first + j * HD : first + (j + 1) * HD] for j in range(group)], axis=0
    )
    for row in range(0, slots, piece):
        block = block_at(row // share, order) ^ me
        start = pl.multiple_of(block * share + row % share, piece)
        values = v_ref[pl.ds(start, piece), head * HD : (head + 1) * HD]
        grad_p = mm(values, da, NN)
        p = p_ref[head, row : row + piece, :].astype(F32)
        grad_s = (p * (grad_p - dot)).astype(BF16)
        total = mm(grad_s, q, NN) * (1.0 / math.sqrt(HD))
        out_ref[row : row + piece, :] = total.astype(BF16)


def key_grads(head, me, probs, cache_v, grad_att_t, att_t, queries, order, n):
    _, slots, wide = probs.shape
    vmem = pl.BlockSpec(memory_space=pltpu.VMEM)
    return pl.pallas_call(
        functools.partial(keys_kernel, head, order, n),
        in_specs=[pl.BlockSpec(memory_space=pltpu.SMEM)] + [vmem] * 5,
        out_specs=vmem,
        out_shape=jax.ShapeDtypeStruct((slots, HD), BF16),
        compiler_params=pltpu.CompilerParams(vmem_limit_bytes=14 * MIB),
        cost_estimate=pl.CostEstimate(
            flops=4 * slots * wide, bytes_accessed=2 * slots * HD, transcendentals=0
        ),
        name="key_grads",
    )(me, probs, cache_v, grad_att_t, att_t, queries)


def squares_kernel(count, *refs):
    parts, (keys_ref, vals_ref, sum_ref) = refs[: 2 * count], refs[2 * count :]
    half = count // 2
    square = None
    for at in range(count):
        own_ref, got_ref = parts[2 * at], parts[2 * at + 1]
        total = own_ref[: got_ref.shape[0], :].astype(F32) + got_ref[...].astype(F32)
        out_ref, head = (vals_ref, at) if at < half else (keys_ref, at - half)
        out_ref[:, head * HD : (head + 1) * HD] = total
        here = jnp.sum((total * total).reshape(-1, 8, HD), axis=0)
        square = here if square is None else square + here
    sum_ref[...] = jnp.broadcast_to(jnp.sum(square, keepdims=True), sum_ref.shape)


def squares(parts, devices):
    flat = [term for pair in parts for term in pair]
    share = flat[1].shape[0]
    count = len(parts)
    vmem = pl.BlockSpec(memory_space=pltpu.VMEM)
    grads = jax.ShapeDtypeStruct((share, count // 2 * HD), F32)
    return pl.pallas_call(
        functools.partial(squares_kernel, count),
        in_specs=[vmem] * len(flat),
        out_specs=[vmem] * 3,
        out_shape=[grads, grads, jax.ShapeDtypeStruct((devices, 128), F32)],
        compiler_params=pltpu.CompilerParams(vmem_limit_bytes=8 * MIB),
        cost_estimate=pl.CostEstimate(
            flops=6 * count * share * HD, bytes_accessed=8 * count * share * HD, transcendentals=0
        ),
        name="squares",
    )(*flat)


def update_kernel(sums_ref, keys_ref, vals_ref, grad_k_ref, grad_v_ref, new_k_ref, new_v_ref):
    total = jnp.sum(sums_ref[...], axis=0, keepdims=True)[:, :1]
    rms = jnp.sqrt(total / (2 * SLOTS * KVH * HD) + epsilon)
    factor = step_rate / rms
    new_k_ref[...] = keys_ref[...].astype(F32) - factor * grad_k_ref[...]
    new_v_ref[...] = vals_ref[...].astype(F32) - factor * grad_v_ref[...]


def update(sums, own_keys, own_vals, grad_k, grad_v):
    vmem = pl.BlockSpec(memory_space=pltpu.VMEM)
    return pl.pallas_call(
        update_kernel,
        in_specs=[vmem] * 5,
        out_specs=[vmem] * 2,
        out_shape=[jax.ShapeDtypeStruct(grad_k.shape, F32)] * 2,
        compiler_params=pltpu.CompilerParams(vmem_limit_bytes=8 * MIB),
        cost_estimate=pl.CostEstimate(
            flops=4 * grad_k.size, bytes_accessed=20 * grad_k.size, transcendentals=0
        ),
        name="update",
    )(sums, own_keys, own_vals, grad_k, grad_v)


def exchange(value, axis, size, flip):
    return lax.ppermute(value, axis, [(i, i ^ flip) for i in range(size)])


def first_halving(part, order, n):
    if not order:
        return part, jnp.zeros_like(part)
    return part, exchange(part[part.shape[0] // 2 :], "dp", n, 1 << order[0])


def rest_halving(part, got, order, n):
    for bit in order[1:]:
        half = got.shape[0]
        part = (part[:half].astype(F32) + got.astype(F32)).astype(BF16)
        got = exchange(part[half // 2 :], "dp", n, 1 << bit)
    return part, got


def body(queries, span_keys, span_values, cache_keys, cache_values, out_proj, out_grad, doc_ids):
    n = lax.axis_size("dp")
    t = lax.axis_size("tensor")
    mine = lax.axis_index("dp")
    shard = lax.axis_index("tensor")
    me = mine.astype(jnp.int32).reshape(1)
    length = queries.shape[0]
    kv = cache_keys.shape[1] // HD
    group = queries.shape[1] // HD // kv
    share = cache_keys.shape[0] // n
    orders = bit_orders(n, kv)

    flips = [2 * s for s in range(1, t // 2)]
    far = [exchange(out_grad, "tensor", t, flip) for flip in flips]
    near = exchange(out_grad, "tensor", t, 1)

    docs = doc_ids[0]
    places = jnp.arange(length)
    span_ok = (docs[None, :] == docs[:, None]) & (places[:, None] <= places[None, :])
    bias = jnp.where(span_ok, 0.0, -1e30).astype(F32)
    probs, attended, att_t, held = forward(
        me, queries, cache_keys, span_keys, cache_values, span_values, bias, out_proj, orders, n
    )
    shard = shard.astype(jnp.int32).reshape(1)
    acc = project(shard, held, out_grad)
    acc = project(shard ^ 1, held, near, acc)
    far, acc = lax.optimization_barrier((far, acc))
    later = [exchange(got, "tensor", t, 1) for got in far]
    for flip, got in zip(flips, far):
        acc = project(shard ^ flip, held, got, acc)
    for flip, got in zip(flips, later):
        acc = project(shard ^ (flip + 1), held, got, acc, group if flip == flips[-1] else 0)

    kernels = [functools.partial(value_grads, h, probs) for h in range(kv)]
    kernels += [
        lambda acc, h=h: key_grads(
            h, me, probs, cache_values, acc, att_t, queries, orders[h], n
        )
        for h in range(kv)
    ]
    parts = []
    for at, kernel in enumerate(kernels):
        grad = kernel(acc)
        if at < len(kernels) - 1:
            acc, grad = lax.optimization_barrier((acc, grad))
        parts.append(first_halving(grad, orders[at % kv], n))
    grads = [rest_halving(*part, orders[at % kv], n) for at, part in enumerate(parts)]
    grad_k, grad_v, sums = squares(grads, n * t)
    sums = lax.all_to_all(sums, ("dp", "tensor"), split_axis=0, concat_axis=0, tiled=True)
    own_keys = lax.dynamic_slice_in_dim(cache_keys, mine * share, share, 0)
    own_vals = lax.dynamic_slice_in_dim(cache_values, mine * share, share, 0)
    new_keys, new_values = update(sums, own_keys, own_vals, grad_k, grad_v)
    return (attended, new_keys, new_values)


def solution(mesh):
    placed = (
        P("dp", "tensor"),
        P("dp", "tensor"),
        P("dp", "tensor"),
        P(None, "tensor"),
        P(None, "tensor"),
        P("tensor", None),
        P("dp", "tensor"),
        P("dp", None),
    )
    return jax.shard_map(
        body,
        mesh=mesh,
        in_specs=placed,
        out_specs=(P("dp", "tensor"), P("dp", "tensor"), P("dp", "tensor")),
        check_vma=False,
    )
```

```python
import functools
import math

import jax
import jax.numpy as jnp
from jax import lax
from jax.experimental import pallas as pl
from jax.experimental.pallas import tpu as pltpu
from jax.sharding import PartitionSpec as P

HD = 128
KVH = 8
SLOTS = 2048

step_rate = 0.25
epsilon = 1e-06

F32 = jnp.float32
BF16 = jnp.bfloat16
NT = (((1,), (1,)), ((), ()))
NN = (((1,), (0,)), ((), ()))
TN = (((0,), (0,)), ((), ()))
MIB = 1 << 20


def mm(a, b, dims):
    return lax.dot_general(a, b, dims, preferred_element_type=F32)


def bit_orders(n):
    first = list(range(n.bit_length() - 1))
    return first, first[1::-1] + first[2:]


def place_of(rel, order):
    place = 0
    for step, bit in enumerate(order):
        place = place + (((rel >> bit) & 1) << (len(order) - 1 - step))
    return place


def block_at(place, order):
    rel = 0
    for step, bit in enumerate(order):
        rel = rel + (((place >> (len(order) - 1 - step)) & 1) << bit)
    return rel


def forward_kernel(
    order, n, me_ref, q_ref, k_ref, ks_ref, v_ref, vs_ref, bias_ref, w_ref,
    p_ref, att_ref, att_t_ref, held_ref, s_ref, sems,
):
    g, j = pl.program_id(0), pl.program_id(1)
    cut = w_ref.shape[0] // 4
    copies = [
        pltpu.make_async_copy(
            w_ref.at[c * cut : (c + 1) * cut], held_ref.at[c * cut : (c + 1) * cut], sems.at[c]
        )
        for c in range(4)
    ]

    @pl.when((g == 0) & (j == 0))
    def _():
        for copy in copies:
            copy.start()

    me = me_ref[0]
    slots = k_ref.shape[0]
    length = q_ref.shape[0]
    share = slots // n
    chunk = 256
    scale = math.log2(math.e) / math.sqrt(HD)
    columns = pl.ds(pl.multiple_of(j * length, length), length)
    q = q_ref[...]
    steps = [(k_ref, v_ref, c, c, chunk) for c in range(0, slots, chunk)]
    steps.append((ks_ref, vs_ref, 0, slots, length))
    high = None
    for keys, _, at, row, size in steps:
        s = mm(keys[at : at + size, :], q, NT) * scale
        if keys is ks_ref:
            s = s + bias_ref[...]
        s_ref[row : row + size, :] = s
        top = jnp.max(s.reshape(size // 8, 8, length), axis=0)
        high = top if high is None else jnp.maximum(high, top)
    high = jnp.max(high, axis=0, keepdims=True)
    total = None
    for _, _, _, row, size in steps:
        e = jnp.exp2(s_ref[row : row + size, :] - high)
        s_ref[row : row + size, :] = e
        part = jnp.sum(e.reshape(size // 8, 8, length), axis=0)
        total = part if total is None else total + part
    inverse = 1.0 / jnp.sum(total, axis=0, keepdims=True)
    att = None
    for keys, values, at, row, size in steps:
        p = (s_ref[row : row + size, :] * inverse).astype(BF16)
        if keys is k_ref:
            piece = min(share, size)
            for b in range(0, size, piece):
                block, inside = (at + b) // share, (at + b) % share
                place = place_of(block ^ me, order)
                start = pl.multiple_of(place * share + inside, piece)
                p_ref[g, pl.ds(start, piece), columns] = p[b : b + piece, :]
        part = mm(values[at : at + size, :], p, TN)
        att = part if att is None else att + part
    att_t_ref[0] = att.astype(BF16)
    att_ref[...] = att.T.astype(BF16)

    @pl.when((g == pl.num_programs(0) - 1) & (j == pl.num_programs(1) - 1))
    def _():
        for copy in copies:
            copy.wait()


def forward(me, queries, cache_k, span_k, cache_v, span_v, bias, weights, order, n):
    length, width = queries.shape
    slots, kv_width = cache_k.shape
    kv = kv_width // HD
    group = width // kv_width
    spec = pltpu.PrefetchScalarGridSpec(
        num_scalar_prefetch=1,
        grid=(kv, group),
        in_specs=[
            pl.BlockSpec((length, HD), lambda g, j, me: (0, g * group + j)),
            pl.BlockSpec((slots, HD), lambda g, j, me: (0, g)),
            pl.BlockSpec((length, HD), lambda g, j, me: (0, g)),
            pl.BlockSpec((slots, HD), lambda g, j, me: (0, g)),
            pl.BlockSpec((length, HD), lambda g, j, me: (0, g)),
            pl.BlockSpec((length, length), lambda g, j, me: (0, 0)),
            pl.BlockSpec(memory_space=pl.ANY),
        ],
        out_specs=[
            pl.BlockSpec(memory_space=pltpu.VMEM),
            pl.BlockSpec((length, HD), lambda g, j, me: (0, g * group + j)),
            pl.BlockSpec((1, HD, length), lambda g, j, me: (g, 0, j)),
            pl.BlockSpec(memory_space=pltpu.VMEM),
        ],
        scratch_shapes=[pltpu.VMEM((slots + length, length), F32), pltpu.SemaphoreType.DMA((4,))],
    )
    return pl.pallas_call(
        functools.partial(forward_kernel, order, n),
        grid_spec=spec,
        out_shape=[
            jax.ShapeDtypeStruct((kv, slots, group * length), BF16),
            jax.ShapeDtypeStruct((length, width), BF16),
            jax.ShapeDtypeStruct((kv, HD, group * length), BF16),
            jax.ShapeDtypeStruct(weights.shape, BF16),
        ],
        compiler_params=pltpu.CompilerParams(vmem_limit_bytes=16 * MIB),
        cost_estimate=pl.CostEstimate(
            flops=4 * width * length * (slots + length),
            bytes_accessed=2 * width // HD * length * slots,
            transcendentals=width // HD * length * (slots + length),
        ),
        name="forward",
    )(me, queries, cache_k, span_k, cache_v, span_v, bias, weights)


def streamed_kernel(shard_ref, w_ref, g_ref, out_ref):
    out_ref[...] = mm(w_ref[...], g_ref[...], NT)


def project_streamed(shard, out_proj, grad):
    rows = out_proj.shape[0]
    length, features = grad.shape
    block = min(256, rows)
    return pl.pallas_call(
        streamed_kernel,
        grid_spec=pltpu.PrefetchScalarGridSpec(
            num_scalar_prefetch=1,
            grid=(rows // block,),
            in_specs=[
                pl.BlockSpec((block, features), lambda m, shard: (m, shard[0])),
                pl.BlockSpec((length, features), lambda m, shard: (0, 0)),
            ],
            out_specs=pl.BlockSpec((block, length), lambda m, shard: (m, 0)),
        ),
        out_shape=jax.ShapeDtypeStruct((rows, length), F32),
        compiler_params=pltpu.CompilerParams(vmem_limit_bytes=46 * MIB),
        cost_estimate=pl.CostEstimate(
            flops=2 * rows * length * features,
            bytes_accessed=2 * rows * features,
            transcendentals=0,
        ),
        name="project_streamed",
    )(shard, out_proj, grad)


def project_kernel(adds, heads, shard_ref, w_ref, g_ref, *refs):
    acc_ref, out_ref = refs if adds else (None, refs[0])
    rows, features = w_ref.shape[0], g_ref.shape[1]
    block = min(256, rows)
    columns = pl.ds(pl.multiple_of(shard_ref[0] * features, features), features)
    for m in range(0, rows, block):
        total = mm(w_ref[m : m + block, columns], g_ref[...], NT)
        if adds:
            total = total + acc_ref[m : m + block, :]
        if not heads:
            out_ref[m : m + block, :] = total
            continue
        length = total.shape[1]
        for b in range(0, block, HD):
            head = (m + b) // HD
            at = head % heads * length
            out_ref[head // heads, :, at : at + length] = total[b : b + HD, :].astype(BF16)


def project(shard, out_proj, grad, acc=None, heads=0):
    rows = out_proj.shape[0]
    length, features = grad.shape
    vmem = pl.BlockSpec(memory_space=pltpu.VMEM)
    args = [shard, out_proj, grad] + ([] if acc is None else [acc])
    if heads:
        out = jax.ShapeDtypeStruct((rows // HD // heads, HD, heads * length), BF16)
    else:
        out = jax.ShapeDtypeStruct((rows, length), F32)
    return pl.pallas_call(
        functools.partial(project_kernel, acc is not None, heads),
        in_specs=[pl.BlockSpec(memory_space=pltpu.SMEM)] + [vmem] * (len(args) - 1),
        out_specs=vmem,
        out_shape=out,
        compiler_params=pltpu.CompilerParams(vmem_limit_bytes=8 * MIB),
        cost_estimate=pl.CostEstimate(
            flops=2 * rows * length * features,
            bytes_accessed=2 * rows * features,
            transcendentals=0,
        ),
        name="project",
    )(*args)


def row_pieces(slots, n, base, order):
    share = slots // n
    size = min(share, 256)
    for row in range(0, slots, size):
        away = block_at(row // share, base)
        yield row, place_of(away, order) * share + row % share, size, away


def values_kernel(head, orders, n, p_ref, da_ref, out_ref):
    da = da_ref[head]
    for row, to, size, _ in row_pieces(p_ref.shape[1], n, *orders):
        out_ref[to : to + size, :] = mm(p_ref[head, row : row + size, :], da, NT).astype(BF16)


def value_grads(head, probs, grad_att_t, orders, n):
    _, slots, wide = probs.shape
    vmem = pl.BlockSpec(memory_space=pltpu.VMEM)
    return pl.pallas_call(
        functools.partial(values_kernel, head, orders, n),
        in_specs=[vmem, vmem],
        out_specs=vmem,
        out_shape=jax.ShapeDtypeStruct((slots, HD), BF16),
        compiler_params=pltpu.CompilerParams(vmem_limit_bytes=14 * MIB),
        cost_estimate=pl.CostEstimate(
            flops=2 * slots * wide, bytes_accessed=2 * slots * HD, transcendentals=0
        ),
        name="value_grads",
    )(probs, grad_att_t)


def keys_kernel(head, orders, n, me_ref, p_ref, v_ref, da_ref, att_ref, q_ref, out_ref):
    me = me_ref[0]
    slots = p_ref.shape[1]
    share = slots // n
    length = q_ref.shape[0]
    group = p_ref.shape[2] // length
    da = da_ref[head]
    dot = jnp.sum(da.astype(F32) * att_ref[head].astype(F32), axis=0, keepdims=True)
    first = head * group * HD
    q = jnp.concatenate(
        [q_ref[:, first + j * HD : first + (j + 1) * HD] for j in range(group)], axis=0
    )
    for row, to, size, away in row_pieces(slots, n, *orders):
        start = pl.multiple_of((away ^ me) * share + row % share, size)
        values = v_ref[pl.ds(start, size), head * HD : (head + 1) * HD]
        grad_p = mm(values, da, NN)
        p = p_ref[head, row : row + size, :].astype(F32)
        grad_s = (p * (grad_p - dot)).astype(BF16)
        total = mm(grad_s, q, NN) * (1.0 / math.sqrt(HD))
        out_ref[to : to + size, :] = total.astype(BF16)


def key_grads(head, me, probs, cache_v, grad_att_t, att_t, queries, orders, n):
    _, slots, wide = probs.shape
    vmem = pl.BlockSpec(memory_space=pltpu.VMEM)
    return pl.pallas_call(
        functools.partial(keys_kernel, head, orders, n),
        in_specs=[pl.BlockSpec(memory_space=pltpu.SMEM)] + [vmem] * 5,
        out_specs=vmem,
        out_shape=jax.ShapeDtypeStruct((slots, HD), BF16),
        compiler_params=pltpu.CompilerParams(vmem_limit_bytes=14 * MIB),
        cost_estimate=pl.CostEstimate(
            flops=4 * slots * wide, bytes_accessed=2 * slots * HD, transcendentals=0
        ),
        name="key_grads",
    )(me, probs, cache_v, grad_att_t, att_t, queries)


def squares_kernel(count, *refs):
    parts, (keys_ref, vals_ref, sum_ref) = refs[: 2 * count], refs[2 * count :]
    half = count // 2
    square = None
    for at in range(count):
        own_ref, got_ref = parts[2 * at], parts[2 * at + 1]
        total = own_ref[: got_ref.shape[0], :].astype(F32) + got_ref[...].astype(F32)
        out_ref, head = (keys_ref, at) if at < half else (vals_ref, at - half)
        out_ref[:, head * HD : (head + 1) * HD] = total
        here = jnp.sum((total * total).reshape(-1, 8, HD), axis=0)
        square = here if square is None else square + here
    sum_ref[...] = jnp.broadcast_to(jnp.sum(square, keepdims=True), sum_ref.shape)


def squares(parts, devices):
    flat = [term for pair in parts for term in pair]
    share = flat[1].shape[0]
    count = len(parts)
    vmem = pl.BlockSpec(memory_space=pltpu.VMEM)
    grads = jax.ShapeDtypeStruct((share, count // 2 * HD), F32)
    return pl.pallas_call(
        functools.partial(squares_kernel, count),
        in_specs=[vmem] * len(flat),
        out_specs=[vmem] * 3,
        out_shape=[grads, grads, jax.ShapeDtypeStruct((devices, 128), F32)],
        compiler_params=pltpu.CompilerParams(vmem_limit_bytes=8 * MIB),
        cost_estimate=pl.CostEstimate(
            flops=6 * count * share * HD, bytes_accessed=8 * count * share * HD, transcendentals=0
        ),
        name="squares",
    )(*flat)


def update_kernel(me_ref, sums_ref, keys_ref, vals_ref, grad_k_ref, grad_v_ref, new_k_ref, new_v_ref):
    total = jnp.sum(sums_ref[...], axis=0, keepdims=True)[:, :1]
    rms = jnp.sqrt(total / (2 * SLOTS * KVH * HD) + epsilon)
    factor = step_rate / rms
    new_k_ref[...] = keys_ref[...].astype(F32) - factor * grad_k_ref[...]
    new_v_ref[...] = vals_ref[...].astype(F32) - factor * grad_v_ref[...]


def update(me, sums, cache_k, cache_v, grad_k, grad_v):
    share, width = grad_k.shape
    own = pl.BlockSpec((share, width), lambda i, me: (me[0], 0))
    whole = pl.BlockSpec((share, width), lambda i, me: (0, 0))
    return pl.pallas_call(
        update_kernel,
        grid_spec=pltpu.PrefetchScalarGridSpec(
            num_scalar_prefetch=1,
            grid=(1,),
            in_specs=[pl.BlockSpec(sums.shape, lambda i, me: (0, 0)), own, own, whole, whole],
            out_specs=[whole, whole],
        ),
        out_shape=[jax.ShapeDtypeStruct(grad_k.shape, F32)] * 2,
        compiler_params=pltpu.CompilerParams(vmem_limit_bytes=8 * MIB),
        cost_estimate=pl.CostEstimate(
            flops=4 * grad_k.size, bytes_accessed=20 * grad_k.size, transcendentals=0
        ),
        name="update",
    )(me, sums, cache_k, cache_v, grad_k, grad_v)


def exchange(value, axis, size, flip):
    return lax.ppermute(value, axis, [(i, i ^ flip) for i in range(size)])


def first_halving(part, order, n):
    if not order:
        return part, jnp.zeros_like(part)
    return part, exchange(part[part.shape[0] // 2 :], "dp", n, 1 << order[0])


def next_halving(part, bit, n):
    rows, got = part
    half = got.shape[0]
    rows = (rows[:half].astype(F32) + got.astype(F32)).astype(BF16)
    return rows, exchange(rows[half // 2 :], "dp", n, 1 << bit)


def in_order(value, part):
    rows, got = part
    if isinstance(value, tuple):
        value_rows, value_got = value
        value_got, got = lax.optimization_barrier((value_got, got))
        return (value_rows, value_got), (rows, got)
    value, got = lax.optimization_barrier((value, got))
    return value, (rows, got)


def body(queries, span_keys, span_values, cache_keys, cache_values, out_proj, out_grad, doc_ids):
    n = lax.axis_size("dp")
    t = lax.axis_size("tensor")
    mine = lax.axis_index("dp")
    shard = lax.axis_index("tensor").astype(jnp.int32).reshape(1)
    me = mine.astype(jnp.int32).reshape(1)
    out_grad, me, shard = lax.optimization_barrier((out_grad, me, shard))
    length = queries.shape[0]
    kv = cache_keys.shape[1] // HD
    group = queries.shape[1] // HD // kv
    base, other = bit_orders(n)

    flips = [2 * s for s in range(1, t // 2)]
    far = [exchange(out_grad, "tensor", t, flip) for flip in flips]
    near = exchange(out_grad, "tensor", t, 1)

    docs = doc_ids[0]
    places = jnp.arange(length)
    span_ok = (docs[None, :] == docs[:, None]) & (places[:, None] <= places[None, :])
    bias = jnp.where(span_ok, 0.0, -1e30).astype(F32)
    acc = project_streamed(shard, out_proj, out_grad)
    me, acc = lax.optimization_barrier((me, acc))
    probs, attended, att_t, held = forward(
        me, queries, cache_keys, span_keys, cache_values, span_values, bias, out_proj, base, n
    )
    acc = project(shard ^ 1, held, near, acc)
    far, acc = lax.optimization_barrier((far, acc))
    later = [exchange(got, "tensor", t, 1) for got in far]
    for flip, got in zip(flips, far):
        acc = project(shard ^ flip, held, got, acc)
    for flip, got in zip(flips, later):
        acc = project(shard ^ (flip + 1), held, got, acc, group if flip == flips[-1] else 0)

    def values(h, acc, order):
        return value_grads(h, probs, acc, (base, order), n)

    def keys(h, acc, order):
        return key_grads(h, me, probs, cache_values, acc, att_t, queries, (base, order), n)

    kernels = [functools.partial(values, h) for h in range(kv)]
    kernels += [functools.partial(keys, h) for h in range(kv)]
    orders = ([base, other, other, base] if kv == 2 else [base] * len(kernels))
    parts = []
    for at, (kernel, order) in enumerate(zip(kernels, orders)):
        final = at == len(kernels) - 1
        grad = kernel(acc, order)
        if final:
            grad, parts[0] = in_order(grad, parts[0])
        parts.append(first_halving(grad, order, n))
    for step in range(1, len(base)):
        for at, order in enumerate(orders):
            parts[at] = next_halving(parts[at], order[step], n)
    grads = parts[kv:] + parts[:kv]
    grad_k, grad_v, sums = squares(grads, n * t)
    sums = lax.all_to_all(sums, ("dp", "tensor"), split_axis=0, concat_axis=0, tiled=True)
    new_keys, new_values = update(me, sums, cache_keys, cache_values, grad_k, grad_v)
    return (attended, new_keys, new_values)


def solution(mesh):
    placed = (
        P("dp", "tensor"),
        P("dp", "tensor"),
        P("dp", "tensor"),
        P(None, "tensor"),
        P(None, "tensor"),
        P("tensor", None),
        P("dp", "tensor"),
        P("dp", None),
    )
    return jax.shard_map(
        body,
        mesh=mesh,
        in_specs=placed,
        out_specs=(P("dp", "tensor"), P("dp", "tensor"), P("dp", "tensor")),
        check_vma=False,
    )
```

```python
import functools
import math

import jax
import jax.numpy as jnp
from jax import lax
from jax.experimental import pallas as pl
from jax.experimental.pallas import tpu as pltpu
from jax.sharding import PartitionSpec as P

HD = 128
KVH = 8
SLOTS = 2048

step_rate = 0.25
epsilon = 1e-06

F32 = jnp.float32
BF16 = jnp.bfloat16
NT = (((1,), (1,)), ((), ()))
NN = (((1,), (0,)), ((), ()))
TN = (((0,), (0,)), ((), ()))
MIB = 1 << 20


def mm(a, b, dims):
    return lax.dot_general(a, b, dims, preferred_element_type=F32)


def bit_orders(n):
    first = list(range(n.bit_length() - 1))
    return first, first[1::-1] + first[2:]


def place_of(rel, order):
    place = 0
    for step, bit in enumerate(order):
        place = place + (((rel >> bit) & 1) << (len(order) - 1 - step))
    return place


def block_at(place, order):
    rel = 0
    for step, bit in enumerate(order):
        rel = rel + (((place >> (len(order) - 1 - step)) & 1) << bit)
    return rel


def forward_kernel(
    order, n, me_ref, q_ref, k_ref, ks_ref, v_ref, vs_ref, bias_ref, w_ref,
    p_ref, att_ref, att_t_ref, held_ref, s_ref, sems,
):
    g, j = pl.program_id(0), pl.program_id(1)
    cut = w_ref.shape[0] // 4
    copies = [
        pltpu.make_async_copy(
            w_ref.at[c * cut : (c + 1) * cut], held_ref.at[c * cut : (c + 1) * cut], sems.at[c]
        )
        for c in range(4)
    ]

    @pl.when((g == 0) & (j == 0))
    def _():
        for copy in copies:
            copy.start()

    me = me_ref[0]
    slots = k_ref.shape[0]
    length = q_ref.shape[0]
    share = slots // n
    chunk = 256
    scale = math.log2(math.e) / math.sqrt(HD)
    columns = pl.ds(pl.multiple_of(j * length, length), length)
    q = q_ref[...]
    steps = [(k_ref, v_ref, c, c, chunk) for c in range(0, slots, chunk)]
    steps.append((ks_ref, vs_ref, 0, slots, length))
    high = None
    for keys, _, at, row, size in steps:
        s = mm(keys[at : at + size, :], q, NT) * scale
        if keys is ks_ref:
            s = s + bias_ref[...]
        s_ref[row : row + size, :] = s
        top = jnp.max(s.reshape(size // 8, 8, length), axis=0)
        high = top if high is None else jnp.maximum(high, top)
    high = jnp.max(high, axis=0, keepdims=True)
    total = None
    for _, _, _, row, size in steps:
        e = jnp.exp2(s_ref[row : row + size, :] - high)
        s_ref[row : row + size, :] = e
        part = jnp.sum(e.reshape(size // 8, 8, length), axis=0)
        total = part if total is None else total + part
    inverse = 1.0 / jnp.sum(total, axis=0, keepdims=True)
    att = None
    for keys, values, at, row, size in steps:
        p = (s_ref[row : row + size, :] * inverse).astype(BF16)
        if keys is k_ref:
            piece = min(share, size)
            for b in range(0, size, piece):
                block, inside = (at + b) // share, (at + b) % share
                place = place_of(block ^ me, order)
                start = pl.multiple_of(place * share + inside, piece)
                p_ref[g, pl.ds(start, piece), columns] = p[b : b + piece, :]
        part = mm(values[at : at + size, :], p, TN)
        att = part if att is None else att + part
    att_t_ref[0] = att.astype(BF16)
    att_ref[...] = att.T.astype(BF16)

    @pl.when((g == pl.num_programs(0) - 1) & (j == pl.num_programs(1) - 1))
    def _():
        for copy in copies:
            copy.wait()


def forward(me, queries, cache_k, span_k, cache_v, span_v, bias, weights, order, n):
    length, width = queries.shape
    slots, kv_width = cache_k.shape
    kv = kv_width // HD
    group = width // kv_width
    spec = pltpu.PrefetchScalarGridSpec(
        num_scalar_prefetch=1,
        grid=(kv, group),
        in_specs=[
            pl.BlockSpec((length, HD), lambda g, j, me: (0, g * group + j)),
            pl.BlockSpec((slots, HD), lambda g, j, me: (0, g)),
            pl.BlockSpec((length, HD), lambda g, j, me: (0, g)),
            pl.BlockSpec((slots, HD), lambda g, j, me: (0, g)),
            pl.BlockSpec((length, HD), lambda g, j, me: (0, g)),
            pl.BlockSpec((length, length), lambda g, j, me: (0, 0)),
            pl.BlockSpec(memory_space=pl.ANY),
        ],
        out_specs=[
            pl.BlockSpec(memory_space=pltpu.VMEM),
            pl.BlockSpec((length, HD), lambda g, j, me: (0, g * group + j)),
            pl.BlockSpec((1, HD, length), lambda g, j, me: (g, 0, j)),
            pl.BlockSpec(memory_space=pltpu.VMEM),
        ],
        scratch_shapes=[pltpu.VMEM((slots + length, length), F32), pltpu.SemaphoreType.DMA((4,))],
    )
    return pl.pallas_call(
        functools.partial(forward_kernel, order, n),
        grid_spec=spec,
        out_shape=[
            jax.ShapeDtypeStruct((kv, slots, group * length), BF16),
            jax.ShapeDtypeStruct((length, width), BF16),
            jax.ShapeDtypeStruct((kv, HD, group * length), BF16),
            jax.ShapeDtypeStruct(weights.shape, BF16),
        ],
        compiler_params=pltpu.CompilerParams(vmem_limit_bytes=16 * MIB),
        cost_estimate=pl.CostEstimate(
            flops=4 * width * length * (slots + length),
            bytes_accessed=2 * width // HD * length * slots,
            transcendentals=width // HD * length * (slots + length),
        ),
        name="forward",
    )(me, queries, cache_k, span_k, cache_v, span_v, bias, weights)


def streamed_kernel(shard_ref, w_ref, g_ref, out_ref):
    out_ref[...] = mm(w_ref[...], g_ref[...], NT)


def project_streamed(shard, out_proj, grad):
    rows = out_proj.shape[0]
    length, features = grad.shape
    block = min(256, rows)
    return pl.pallas_call(
        streamed_kernel,
        grid_spec=pltpu.PrefetchScalarGridSpec(
            num_scalar_prefetch=1,
            grid=(rows // block,),
            in_specs=[
                pl.BlockSpec((block, features), lambda m, shard: (m, shard[0])),
                pl.BlockSpec((length, features), lambda m, shard: (0, 0)),
            ],
            out_specs=pl.BlockSpec((block, length), lambda m, shard: (m, 0)),
        ),
        out_shape=jax.ShapeDtypeStruct((rows, length), F32),
        compiler_params=pltpu.CompilerParams(vmem_limit_bytes=46 * MIB),
        cost_estimate=pl.CostEstimate(
            flops=2 * rows * length * features,
            bytes_accessed=2 * rows * features,
            transcendentals=0,
        ),
        name="project_streamed",
    )(shard, out_proj, grad)


def project_kernel(adds, heads, shard_ref, w_ref, g_ref, *refs):
    acc_ref, out_ref = refs if adds else (None, refs[0])
    rows, features = w_ref.shape[0], g_ref.shape[1]
    block = min(256, rows)
    columns = pl.ds(pl.multiple_of(shard_ref[0] * features, features), features)
    for m in range(0, rows, block):
        total = mm(w_ref[m : m + block, columns], g_ref[...], NT)
        if adds:
            total = total + acc_ref[m : m + block, :]
        if not heads:
            out_ref[m : m + block, :] = total
            continue
        length = total.shape[1]
        for b in range(0, block, HD):
            head = (m + b) // HD
            at = head % heads * length
            out_ref[head // heads, :, at : at + length] = total[b : b + HD, :].astype(BF16)


def project(shard, out_proj, grad, acc=None, heads=0):
    rows = out_proj.shape[0]
    length, features = grad.shape
    vmem = pl.BlockSpec(memory_space=pltpu.VMEM)
    args = [shard, out_proj, grad] + ([] if acc is None else [acc])
    if heads:
        out = jax.ShapeDtypeStruct((rows // HD // heads, HD, heads * length), BF16)
    else:
        out = jax.ShapeDtypeStruct((rows, length), F32)
    return pl.pallas_call(
        functools.partial(project_kernel, acc is not None, heads),
        in_specs=[pl.BlockSpec(memory_space=pltpu.SMEM)] + [vmem] * (len(args) - 1),
        out_specs=vmem,
        out_shape=out,
        compiler_params=pltpu.CompilerParams(vmem_limit_bytes=8 * MIB),
        cost_estimate=pl.CostEstimate(
            flops=2 * rows * length * features,
            bytes_accessed=2 * rows * features,
            transcendentals=0,
        ),
        name="project",
    )(*args)


def row_pieces(slots, n, base, order, side):
    share = slots // n
    size = min(share, 256)
    for row in range(0, slots, size):
        away = block_at(row // share, base)
        to = place_of(away, order) * share + row % share - side * (slots // 2)
        if 0 <= to < slots // 2:
            yield row, to, size, away


def values_kernel(head, layout, n, p_ref, da_ref, out_ref):
    da = da_ref[head]
    for row, to, size, _ in row_pieces(p_ref.shape[1], n, *layout):
        out_ref[to : to + size, :] = mm(p_ref[head, row : row + size, :], da, NT).astype(BF16)


def value_grads(head, probs, grad_att_t, layout, n):
    _, slots, wide = probs.shape
    vmem = pl.BlockSpec(memory_space=pltpu.VMEM)
    return pl.pallas_call(
        functools.partial(values_kernel, head, layout, n),
        in_specs=[vmem, vmem],
        out_specs=vmem,
        out_shape=jax.ShapeDtypeStruct((slots // 2, HD), BF16),
        compiler_params=pltpu.CompilerParams(vmem_limit_bytes=14 * MIB),
        cost_estimate=pl.CostEstimate(
            flops=2 * slots * wide, bytes_accessed=2 * slots * HD, transcendentals=0
        ),
        name="value_grads",
    )(probs, grad_att_t)


def keys_kernel(head, layout, n, me_ref, p_ref, v_ref, da_ref, att_ref, q_ref, out_ref):
    me = me_ref[0]
    slots = p_ref.shape[1]
    share = slots // n
    length = q_ref.shape[0]
    group = p_ref.shape[2] // length
    da = da_ref[head]
    dot = jnp.sum(da.astype(F32) * att_ref[head].astype(F32), axis=0, keepdims=True)
    first = head * group * HD
    q = jnp.concatenate(
        [q_ref[:, first + j * HD : first + (j + 1) * HD] for j in range(group)], axis=0
    )
    for row, to, size, away in row_pieces(slots, n, *layout):
        start = pl.multiple_of((away ^ me) * share + row % share, size)
        values = v_ref[pl.ds(start, size), head * HD : (head + 1) * HD]
        grad_p = mm(values, da, NN)
        p = p_ref[head, row : row + size, :].astype(F32)
        grad_s = (p * (grad_p - dot)).astype(BF16)
        total = mm(grad_s, q, NN) * (1.0 / math.sqrt(HD))
        out_ref[to : to + size, :] = total.astype(BF16)


def key_grads(head, me, probs, cache_v, grad_att_t, att_t, queries, layout, n):
    _, slots, wide = probs.shape
    vmem = pl.BlockSpec(memory_space=pltpu.VMEM)
    return pl.pallas_call(
        functools.partial(keys_kernel, head, layout, n),
        in_specs=[pl.BlockSpec(memory_space=pltpu.SMEM)] + [vmem] * 5,
        out_specs=vmem,
        out_shape=jax.ShapeDtypeStruct((slots // 2, HD), BF16),
        compiler_params=pltpu.CompilerParams(vmem_limit_bytes=14 * MIB),
        cost_estimate=pl.CostEstimate(
            flops=4 * slots * wide, bytes_accessed=2 * slots * HD, transcendentals=0
        ),
        name="key_grads",
    )(me, probs, cache_v, grad_att_t, att_t, queries)


def squares_kernel(count, *refs):
    parts, (keys_ref, vals_ref, sum_ref) = refs[: 2 * count], refs[2 * count :]
    half = count // 2
    square = None
    for at in range(count):
        own_ref, got_ref = parts[2 * at], parts[2 * at + 1]
        total = own_ref[: got_ref.shape[0], :].astype(F32) + got_ref[...].astype(F32)
        out_ref, head = (keys_ref, at) if at < half else (vals_ref, at - half)
        out_ref[:, head * HD : (head + 1) * HD] = total
        here = jnp.sum((total * total).reshape(-1, 8, HD), axis=0)
        square = here if square is None else square + here
    sum_ref[...] = jnp.broadcast_to(jnp.sum(square, keepdims=True), sum_ref.shape)


def squares(parts, devices):
    flat = [term for pair in parts for term in pair]
    share = flat[1].shape[0]
    count = len(parts)
    vmem = pl.BlockSpec(memory_space=pltpu.VMEM)
    grads = jax.ShapeDtypeStruct((share, count // 2 * HD), F32)
    return pl.pallas_call(
        functools.partial(squares_kernel, count),
        in_specs=[vmem] * len(flat),
        out_specs=[vmem] * 3,
        out_shape=[grads, grads, jax.ShapeDtypeStruct((devices, 128), F32)],
        compiler_params=pltpu.CompilerParams(vmem_limit_bytes=8 * MIB),
        cost_estimate=pl.CostEstimate(
            flops=6 * count * share * HD, bytes_accessed=8 * count * share * HD, transcendentals=0
        ),
        name="squares",
    )(*flat)


def update_kernel(me_ref, sums_ref, keys_ref, vals_ref, grad_k_ref, grad_v_ref, new_k_ref, new_v_ref):
    total = jnp.sum(sums_ref[...], axis=0, keepdims=True)[:, :1]
    rms = jnp.sqrt(total / (2 * SLOTS * KVH * HD) + epsilon)
    factor = step_rate / rms
    new_k_ref[...] = keys_ref[...].astype(F32) - factor * grad_k_ref[...]
    new_v_ref[...] = vals_ref[...].astype(F32) - factor * grad_v_ref[...]


def update(me, sums, cache_k, cache_v, grad_k, grad_v):
    share, width = grad_k.shape
    own = pl.BlockSpec((share, width), lambda i, me: (me[0], 0))
    whole = pl.BlockSpec((share, width), lambda i, me: (0, 0))
    return pl.pallas_call(
        update_kernel,
        grid_spec=pltpu.PrefetchScalarGridSpec(
            num_scalar_prefetch=1,
            grid=(1,),
            in_specs=[pl.BlockSpec(sums.shape, lambda i, me: (0, 0)), own, own, whole, whole],
            out_specs=[whole, whole],
        ),
        out_shape=[jax.ShapeDtypeStruct(grad_k.shape, F32)] * 2,
        compiler_params=pltpu.CompilerParams(vmem_limit_bytes=8 * MIB),
        cost_estimate=pl.CostEstimate(
            flops=4 * grad_k.size, bytes_accessed=20 * grad_k.size, transcendentals=0
        ),
        name="update",
    )(me, sums, cache_k, cache_v, grad_k, grad_v)


def exchange(value, axis, size, flip):
    return lax.ppermute(value, axis, [(i, i ^ flip) for i in range(size)])


def next_halving(part, bit, n):
    rows, got = part
    half = got.shape[0]
    rows = (rows[:half].astype(F32) + got.astype(F32)).astype(BF16)
    return rows, exchange(rows[half // 2 :], "dp", n, 1 << bit)


def in_order(value, part):
    rows, got = part
    if isinstance(value, tuple):
        value_rows, value_got = value
        value_got, got = lax.optimization_barrier((value_got, got))
        return (value_rows, value_got), (rows, got)
    value, got = lax.optimization_barrier((value, got))
    return value, (rows, got)


def body(queries, span_keys, span_values, cache_keys, cache_values, out_proj, out_grad, doc_ids):
    n = lax.axis_size("dp")
    t = lax.axis_size("tensor")
    mine = lax.axis_index("dp")
    shard = lax.axis_index("tensor").astype(jnp.int32).reshape(1)
    me = mine.astype(jnp.int32).reshape(1)
    out_grad, me, shard = lax.optimization_barrier((out_grad, me, shard))
    length = queries.shape[0]
    kv = cache_keys.shape[1] // HD
    group = queries.shape[1] // HD // kv
    base, other = bit_orders(n)

    flips = [2 * s for s in range(1, t // 2)]
    far = [exchange(out_grad, "tensor", t, flip) for flip in flips]
    near = exchange(out_grad, "tensor", t, 1)

    docs = doc_ids[0]
    places = jnp.arange(length)
    span_ok = (docs[None, :] == docs[:, None]) & (places[:, None] <= places[None, :])
    bias = jnp.where(span_ok, 0.0, -1e30).astype(F32)
    acc = project_streamed(shard, out_proj, out_grad)
    me, acc = lax.optimization_barrier((me, acc))
    probs, attended, att_t, held = forward(
        me, queries, cache_keys, span_keys, cache_values, span_values, bias, out_proj, base, n
    )
    acc = project(shard ^ 1, held, near, acc)
    far, acc = lax.optimization_barrier((far, acc))
    later = [exchange(got, "tensor", t, 1) for got in far]
    for flip, got in zip(flips, far):
        acc = project(shard ^ flip, held, got, acc)
    for flip, got in zip(flips, later):
        acc = project(shard ^ (flip + 1), held, got, acc, group if flip == flips[-1] else 0)

    def values(h, acc, order, side):
        return value_grads(h, probs, acc, (base, order, side), n)

    def keys(h, acc, order, side):
        return key_grads(h, me, probs, cache_values, acc, att_t, queries, (base, order, side), n)

    kernels = [functools.partial(values, h) for h in range(kv)]
    kernels += [functools.partial(keys, h) for h in range(kv)]
    orders = [base, other, other, base] if kv == 2 else [base] * len(kernels)
    got = []
    for kernel, order in zip(kernels, orders):
        sent = kernel(acc, order, 1)
        acc, sent = lax.optimization_barrier((acc, sent))
        got.append(exchange(sent, "dp", n, 1 << order[0]))
    parts = []
    for at, (kernel, order) in enumerate(zip(kernels, orders)):
        if at == 1:
            acc, got[0] = lax.optimization_barrier((acc, got[0]))
            parts[0] = (parts[0][0], got[0])
        parts.append((kernel(acc, order, 0), got[at]))
    for step in range(1, len(base)):
        for at, order in enumerate(orders):
            parts[at] = next_halving(parts[at], order[step], n)
    grads = parts[kv:] + parts[:kv]
    grad_k, grad_v, sums = squares(grads, n * t)
    sums = lax.all_to_all(sums, ("dp", "tensor"), split_axis=0, concat_axis=0, tiled=True)
    new_keys, new_values = update(me, sums, cache_keys, cache_values, grad_k, grad_v)
    return (attended, new_keys, new_values)


def solution(mesh):
    placed = (
        P("dp", "tensor"),
        P("dp", "tensor"),
        P("dp", "tensor"),
        P(None, "tensor"),
        P(None, "tensor"),
        P("tensor", None),
        P("dp", "tensor"),
        P("dp", None),
    )
    return jax.shard_map(
        body,
        mesh=mesh,
        in_specs=placed,
        out_specs=(P("dp", "tensor"), P("dp", "tensor"), P("dp", "tensor")),
        check_vma=False,
    )
```

```python
import functools
import math

import jax
import jax.numpy as jnp
from jax import lax
from jax.experimental import pallas as pl
from jax.experimental.pallas import tpu as pltpu
from jax.sharding import PartitionSpec as P

HD = 128
KVH = 8
SLOTS = 2048

step_rate = 0.25
epsilon = 1e-06

F32 = jnp.float32
BF16 = jnp.bfloat16
NT = (((1,), (1,)), ((), ()))
NN = (((1,), (0,)), ((), ()))
TN = (((0,), (0,)), ((), ()))
MIB = 1 << 20


def mm(a, b, dims):
    return lax.dot_general(a, b, dims, preferred_element_type=F32)


def bit_orders(n):
    first = list(range(n.bit_length() - 1))
    return first, first[1::-1] + first[2:], first[:1] + first[2:0:-1] + first[3:]


def place_of(rel, order):
    place = 0
    for step, bit in enumerate(order):
        place = place + (((rel >> bit) & 1) << (len(order) - 1 - step))
    return place


def block_at(place, order):
    rel = 0
    for step, bit in enumerate(order):
        rel = rel + (((place >> (len(order) - 1 - step)) & 1) << bit)
    return rel


def forward_kernel(
    order, n, me_ref, q_ref, k_ref, ks_ref, v_ref, vs_ref, bias_ref, w_ref,
    p_ref, att_ref, att_t_ref, held_ref, s_ref, sems,
):
    g, j = pl.program_id(0), pl.program_id(1)
    cut = w_ref.shape[0] // 4
    copies = [
        pltpu.make_async_copy(
            w_ref.at[c * cut : (c + 1) * cut], held_ref.at[c * cut : (c + 1) * cut], sems.at[c]
        )
        for c in range(4)
    ]

    @pl.when((g == 0) & (j == 0))
    def _():
        for copy in copies:
            copy.start()

    me = me_ref[0]
    slots = k_ref.shape[0]
    length = q_ref.shape[0]
    share = slots // n
    chunk = 256
    scale = math.log2(math.e) / math.sqrt(HD)
    columns = pl.ds(pl.multiple_of(j * length, length), length)
    q = q_ref[...]
    steps = [(k_ref, v_ref, c, c, chunk) for c in range(0, slots, chunk)]
    steps.append((ks_ref, vs_ref, 0, slots, length))
    high = None
    for keys, _, at, row, size in steps:
        s = mm(keys[at : at + size, :], q, NT) * scale
        if keys is ks_ref:
            s = s + bias_ref[...]
        s_ref[row : row + size, :] = s
        top = jnp.max(s.reshape(size // 8, 8, length), axis=0)
        high = top if high is None else jnp.maximum(high, top)
    high = jnp.max(high, axis=0, keepdims=True)
    total = None
    for _, _, _, row, size in steps:
        e = jnp.exp2(s_ref[row : row + size, :] - high)
        s_ref[row : row + size, :] = e
        part = jnp.sum(e.reshape(size // 8, 8, length), axis=0)
        total = part if total is None else total + part
    inverse = 1.0 / jnp.sum(total, axis=0, keepdims=True)
    att = None
    for keys, values, at, row, size in steps:
        p = (s_ref[row : row + size, :] * inverse).astype(BF16)
        if keys is k_ref:
            piece = min(share, size)
            for b in range(0, size, piece):
                block, inside = (at + b) // share, (at + b) % share
                place = place_of(block ^ me, order)
                start = pl.multiple_of(place * share + inside, piece)
                p_ref[g, pl.ds(start, piece), columns] = p[b : b + piece, :]
        part = mm(values[at : at + size, :], p, TN)
        att = part if att is None else att + part
    att_t_ref[0] = att.astype(BF16)
    att_ref[...] = att.T.astype(BF16)

    @pl.when((g == pl.num_programs(0) - 1) & (j == pl.num_programs(1) - 1))
    def _():
        for copy in copies:
            copy.wait()


def forward(me, queries, cache_k, span_k, cache_v, span_v, bias, weights, order, n):
    length, width = queries.shape
    slots, kv_width = cache_k.shape
    kv = kv_width // HD
    group = width // kv_width
    spec = pltpu.PrefetchScalarGridSpec(
        num_scalar_prefetch=1,
        grid=(kv, group),
        in_specs=[
            pl.BlockSpec((length, HD), lambda g, j, me: (0, g * group + j)),
            pl.BlockSpec((slots, HD), lambda g, j, me: (0, g)),
            pl.BlockSpec((length, HD), lambda g, j, me: (0, g)),
            pl.BlockSpec((slots, HD), lambda g, j, me: (0, g)),
            pl.BlockSpec((length, HD), lambda g, j, me: (0, g)),
            pl.BlockSpec((length, length), lambda g, j, me: (0, 0)),
            pl.BlockSpec(memory_space=pl.ANY),
        ],
        out_specs=[
            pl.BlockSpec(memory_space=pltpu.VMEM),
            pl.BlockSpec((length, HD), lambda g, j, me: (0, g * group + j)),
            pl.BlockSpec((1, HD, length), lambda g, j, me: (g, 0, j)),
            pl.BlockSpec(memory_space=pltpu.VMEM),
        ],
        scratch_shapes=[pltpu.VMEM((slots + length, length), F32), pltpu.SemaphoreType.DMA((4,))],
    )
    return pl.pallas_call(
        functools.partial(forward_kernel, order, n),
        grid_spec=spec,
        out_shape=[
            jax.ShapeDtypeStruct((kv, slots, group * length), BF16),
            jax.ShapeDtypeStruct((length, width), BF16),
            jax.ShapeDtypeStruct((kv, HD, group * length), BF16),
            jax.ShapeDtypeStruct(weights.shape, BF16),
        ],
        compiler_params=pltpu.CompilerParams(vmem_limit_bytes=16 * MIB),
        cost_estimate=pl.CostEstimate(
            flops=4 * width * length * (slots + length),
            bytes_accessed=2 * width // HD * length * slots,
            transcendentals=width // HD * length * (slots + length),
        ),
        name="forward",
    )(me, queries, cache_k, span_k, cache_v, span_v, bias, weights)


def streamed_kernel(shard_ref, w_ref, g_ref, out_ref):
    out_ref[...] = mm(w_ref[...], g_ref[...], NT)


def project_streamed(shard, out_proj, grad):
    rows = out_proj.shape[0]
    length, features = grad.shape
    block = min(256, rows)
    return pl.pallas_call(
        streamed_kernel,
        grid_spec=pltpu.PrefetchScalarGridSpec(
            num_scalar_prefetch=1,
            grid=(rows // block,),
            in_specs=[
                pl.BlockSpec((block, features), lambda m, shard: (m, shard[0])),
                pl.BlockSpec((length, features), lambda m, shard: (0, 0)),
            ],
            out_specs=pl.BlockSpec((block, length), lambda m, shard: (m, 0)),
        ),
        out_shape=jax.ShapeDtypeStruct((rows, length), F32),
        compiler_params=pltpu.CompilerParams(vmem_limit_bytes=46 * MIB),
        cost_estimate=pl.CostEstimate(
            flops=2 * rows * length * features,
            bytes_accessed=2 * rows * features,
            transcendentals=0,
        ),
        name="project_streamed",
    )(shard, out_proj, grad)


def project_kernel(adds, heads, shard_ref, w_ref, g_ref, *refs):
    acc_ref, out_ref = refs if adds else (None, refs[0])
    rows, features = w_ref.shape[0], g_ref.shape[1]
    block = min(256, rows)
    columns = pl.ds(pl.multiple_of(shard_ref[0] * features, features), features)
    for m in range(0, rows, block):
        total = mm(w_ref[m : m + block, columns], g_ref[...], NT)
        if adds:
            total = total + acc_ref[m : m + block, :]
        if not heads:
            out_ref[m : m + block, :] = total
            continue
        length = total.shape[1]
        for b in range(0, block, HD):
            head = (m + b) // HD
            at = head % heads * length
            out_ref[head // heads, :, at : at + length] = total[b : b + HD, :].astype(BF16)


def project(shard, out_proj, grad, acc=None, heads=0):
    rows = out_proj.shape[0]
    length, features = grad.shape
    vmem = pl.BlockSpec(memory_space=pltpu.VMEM)
    args = [shard, out_proj, grad] + ([] if acc is None else [acc])
    if heads:
        out = jax.ShapeDtypeStruct((rows // HD // heads, HD, heads * length), BF16)
    else:
        out = jax.ShapeDtypeStruct((rows, length), F32)
    return pl.pallas_call(
        functools.partial(project_kernel, acc is not None, heads),
        in_specs=[pl.BlockSpec(memory_space=pltpu.SMEM)] + [vmem] * (len(args) - 1),
        out_specs=vmem,
        out_shape=out,
        compiler_params=pltpu.CompilerParams(vmem_limit_bytes=8 * MIB),
        cost_estimate=pl.CostEstimate(
            flops=2 * rows * length * features,
            bytes_accessed=2 * rows * features,
            transcendentals=0,
        ),
        name="project",
    )(*args)


def row_pieces(slots, n, base, order, side):
    share = slots // n
    size = min(share, 256)
    for row in range(0, slots, size):
        away = block_at(row // share, base)
        to = place_of(away, order) * share + row % share - side * (slots // 2)
        if 0 <= to < slots // 2:
            yield row, to, size, away


def values_kernel(head, layout, n, p_ref, da_ref, out_ref):
    da = da_ref[head]
    for row, to, size, _ in row_pieces(p_ref.shape[1], n, *layout):
        out_ref[to : to + size, :] = mm(p_ref[head, row : row + size, :], da, NT).astype(BF16)


def value_grads(head, probs, grad_att_t, layout, n):
    _, slots, wide = probs.shape
    vmem = pl.BlockSpec(memory_space=pltpu.VMEM)
    return pl.pallas_call(
        functools.partial(values_kernel, head, layout, n),
        in_specs=[vmem, vmem],
        out_specs=vmem,
        out_shape=jax.ShapeDtypeStruct((slots // 2, HD), BF16),
        compiler_params=pltpu.CompilerParams(vmem_limit_bytes=14 * MIB),
        cost_estimate=pl.CostEstimate(
            flops=2 * slots * wide, bytes_accessed=2 * slots * HD, transcendentals=0
        ),
        name="value_grads",
    )(probs, grad_att_t)


def keys_kernel(head, layout, n, me_ref, p_ref, v_ref, da_ref, att_ref, q_ref, out_ref):
    me = me_ref[0]
    slots = p_ref.shape[1]
    share = slots // n
    length = q_ref.shape[0]
    group = p_ref.shape[2] // length
    da = da_ref[head]
    dot = jnp.sum(da.astype(F32) * att_ref[head].astype(F32), axis=0, keepdims=True)
    first = head * group * HD
    q = jnp.concatenate(
        [q_ref[:, first + j * HD : first + (j + 1) * HD] for j in range(group)], axis=0
    )
    for row, to, size, away in row_pieces(slots, n, *layout):
        start = pl.multiple_of((away ^ me) * share + row % share, size)
        values = v_ref[pl.ds(start, size), head * HD : (head + 1) * HD]
        grad_p = mm(values, da, NN)
        p = p_ref[head, row : row + size, :].astype(F32)
        grad_s = (p * (grad_p - dot)).astype(BF16)
        total = mm(grad_s, q, NN) * (1.0 / math.sqrt(HD))
        out_ref[to : to + size, :] = total.astype(BF16)


def key_grads(head, me, probs, cache_v, grad_att_t, att_t, queries, layout, n):
    _, slots, wide = probs.shape
    vmem = pl.BlockSpec(memory_space=pltpu.VMEM)
    return pl.pallas_call(
        functools.partial(keys_kernel, head, layout, n),
        in_specs=[pl.BlockSpec(memory_space=pltpu.SMEM)] + [vmem] * 5,
        out_specs=vmem,
        out_shape=jax.ShapeDtypeStruct((slots // 2, HD), BF16),
        compiler_params=pltpu.CompilerParams(vmem_limit_bytes=14 * MIB),
        cost_estimate=pl.CostEstimate(
            flops=4 * slots * wide, bytes_accessed=2 * slots * HD, transcendentals=0
        ),
        name="key_grads",
    )(me, probs, cache_v, grad_att_t, att_t, queries)


def squares_kernel(count, *refs):
    parts, (keys_ref, vals_ref, sum_ref) = refs[: 2 * count], refs[2 * count :]
    half = count // 2
    square = None
    for at in range(count):
        own_ref, got_ref = parts[2 * at], parts[2 * at + 1]
        total = own_ref[: got_ref.shape[0], :].astype(F32) + got_ref[...].astype(F32)
        out_ref, head = (keys_ref, at) if at < half else (vals_ref, at - half)
        out_ref[:, head * HD : (head + 1) * HD] = total
        here = jnp.sum((total * total).reshape(-1, 8, HD), axis=0)
        square = here if square is None else square + here
    sum_ref[...] = jnp.broadcast_to(jnp.sum(square, keepdims=True), sum_ref.shape)


def squares(parts, devices):
    flat = [term for pair in parts for term in pair]
    share = flat[1].shape[0]
    count = len(parts)
    vmem = pl.BlockSpec(memory_space=pltpu.VMEM)
    grads = jax.ShapeDtypeStruct((share, count // 2 * HD), F32)
    return pl.pallas_call(
        functools.partial(squares_kernel, count),
        in_specs=[vmem] * len(flat),
        out_specs=[vmem] * 3,
        out_shape=[grads, grads, jax.ShapeDtypeStruct((devices, 128), F32)],
        compiler_params=pltpu.CompilerParams(vmem_limit_bytes=8 * MIB),
        cost_estimate=pl.CostEstimate(
            flops=6 * count * share * HD, bytes_accessed=8 * count * share * HD, transcendentals=0
        ),
        name="squares",
    )(*flat)


def update_kernel(me_ref, sums_ref, keys_ref, vals_ref, grad_k_ref, grad_v_ref, new_k_ref, new_v_ref):
    total = jnp.sum(sums_ref[...], axis=0, keepdims=True)[:, :1]
    rms = jnp.sqrt(total / (2 * SLOTS * KVH * HD) + epsilon)
    factor = step_rate / rms
    new_k_ref[...] = keys_ref[...].astype(F32) - factor * grad_k_ref[...]
    new_v_ref[...] = vals_ref[...].astype(F32) - factor * grad_v_ref[...]


def update(me, sums, cache_k, cache_v, grad_k, grad_v):
    share, width = grad_k.shape
    own = pl.BlockSpec((share, width), lambda i, me: (me[0], 0))
    whole = pl.BlockSpec((share, width), lambda i, me: (0, 0))
    return pl.pallas_call(
        update_kernel,
        grid_spec=pltpu.PrefetchScalarGridSpec(
            num_scalar_prefetch=1,
            grid=(1,),
            in_specs=[pl.BlockSpec(sums.shape, lambda i, me: (0, 0)), own, own, whole, whole],
            out_specs=[whole, whole],
        ),
        out_shape=[jax.ShapeDtypeStruct(grad_k.shape, F32)] * 2,
        compiler_params=pltpu.CompilerParams(vmem_limit_bytes=8 * MIB),
        cost_estimate=pl.CostEstimate(
            flops=4 * grad_k.size, bytes_accessed=20 * grad_k.size, transcendentals=0
        ),
        name="update",
    )(me, sums, cache_k, cache_v, grad_k, grad_v)


def exchange(value, axis, size, flip):
    return lax.ppermute(value, axis, [(i, i ^ flip) for i in range(size)])


def next_halving(part, bit, n):
    rows, got = part
    half = got.shape[0]
    rows = (rows[:half].astype(F32) + got.astype(F32)).astype(BF16)
    return rows, exchange(rows[half // 2 :], "dp", n, 1 << bit)


def in_order(value, part):
    rows, got = part
    if isinstance(value, tuple):
        value_rows, value_got = value
        value_got, got = lax.optimization_barrier((value_got, got))
        return (value_rows, value_got), (rows, got)
    value, got = lax.optimization_barrier((value, got))
    return value, (rows, got)


def body(queries, span_keys, span_values, cache_keys, cache_values, out_proj, out_grad, doc_ids):
    n = lax.axis_size("dp")
    t = lax.axis_size("tensor")
    mine = lax.axis_index("dp")
    shard = lax.axis_index("tensor").astype(jnp.int32).reshape(1)
    me = mine.astype(jnp.int32).reshape(1)
    out_grad, me, shard = lax.optimization_barrier((out_grad, me, shard))
    length = queries.shape[0]
    kv = cache_keys.shape[1] // HD
    group = queries.shape[1] // HD // kv
    base, other, third = bit_orders(n)

    flips = [2 * s for s in range(1, t // 2)]
    far = [exchange(out_grad, "tensor", t, flip) for flip in flips]
    near = exchange(out_grad, "tensor", t, 1)

    docs = doc_ids[0]
    places = jnp.arange(length)
    span_ok = (docs[None, :] == docs[:, None]) & (places[:, None] <= places[None, :])
    bias = jnp.where(span_ok, 0.0, -1e30).astype(F32)
    acc = project_streamed(shard, out_proj, out_grad)
    me, acc = lax.optimization_barrier((me, acc))
    probs, attended, att_t, held = forward(
        me, queries, cache_keys, span_keys, cache_values, span_values, bias, out_proj, base, n
    )
    acc = project(shard ^ 1, held, near, acc)
    far, acc = lax.optimization_barrier((far, acc))
    later = [exchange(got, "tensor", t, 1) for got in far]
    for flip, got in zip(flips, far):
        acc = project(shard ^ flip, held, got, acc)
    for flip, got in zip(flips, later):
        acc = project(shard ^ (flip + 1), held, got, acc, group if flip == flips[-1] else 0)

    def values(h, acc, order, side):
        return value_grads(h, probs, acc, (base, order, side), n)

    def keys(h, acc, order, side):
        return key_grads(h, me, probs, cache_values, acc, att_t, queries, (base, order, side), n)

    kernels = [functools.partial(values, h) for h in range(kv)]
    kernels += [functools.partial(keys, h) for h in range(kv)]
    orders = [third, other, other, base] if kv == 2 else [base] * len(kernels)
    got = []
    for kernel, order in zip(kernels, orders):
        sent = kernel(acc, order, 1)
        acc, sent = lax.optimization_barrier((acc, sent))
        got.append(exchange(sent, "dp", n, 1 << order[0]))
    parts = []
    for at, (kernel, order) in enumerate(zip(kernels, orders)):
        if at == 1:
            acc, got[0] = lax.optimization_barrier((acc, got[0]))
            parts[0] = (parts[0][0], got[0])
        parts.append((kernel(acc, order, 0), got[at]))
    for step in range(1, len(base)):
        for at, order in enumerate(orders):
            parts[at] = next_halving(parts[at], order[step], n)
    grads = parts[kv:] + parts[:kv]
    grad_k, grad_v, sums = squares(grads, n * t)
    sums = lax.all_to_all(sums, ("dp", "tensor"), split_axis=0, concat_axis=0, tiled=True)
    new_keys, new_values = update(me, sums, cache_keys, cache_values, grad_k, grad_v)
    return (attended, new_keys, new_values)


def solution(mesh):
    placed = (
        P("dp", "tensor"),
        P("dp", "tensor"),
        P("dp", "tensor"),
        P(None, "tensor"),
        P(None, "tensor"),
        P("tensor", None),
        P("dp", "tensor"),
        P("dp", None),
    )
    return jax.shard_map(
        body,
        mesh=mesh,
        in_specs=placed,
        out_specs=(P("dp", "tensor"), P("dp", "tensor"), P("dp", "tensor")),
        check_vma=False,
    )
```
